256 devices in a mesh: inp: 4 (over z_lo), wt: 8 (over z_hi, y), out: 8 (over x, core).
Axes of the slice: x: 4, y: 4, z: 8 (z_hi: 2, z_lo: 4; z = z_hi * 4 + z_lo), core: 2. Of those that a mesh axis runs over, the one named last changes fastest.
Arguments:
- tokens: bfloat16 [512, 12288], P(('wt', 'out'), 'inp'), may hold values from -6 to 6
- weight_in: bfloat16 [12288, 24576], P('inp', ('wt', 'out')), may hold values from -0.0546875 to 0.0546875
- weight_out: bfloat16 [24576, 12288], P(('wt', 'out'), 'inp'), may hold values from -0.0390625 to 0.0390625
- cotangent: bfloat16 [512, 12288], P(('wt', 'out'), 'inp'), may hold values from -6 to 6
Outputs:
- grad_tokens: bfloat16 [512, 12288], P(('wt', 'out'), 'inp')
- grad_weight_in: bfloat16 [12288, 24576], P('inp', ('wt', 'out'))
- grad_weight_out: bfloat16 [24576, 12288], P(('wt', 'out'), 'inp')
The draws below stay inside these ranges and needn't reach their ends.
All inputs are finite; a program needn't handle non-finite values.
Results may differ from the reference program's by a relative error of at most 0.02.
Values may be sent and summed in bfloat16 or wider, within the bound.
No kernel may reach another device: no remote copies, remote signals or barrier semaphores. Data moves between devices by JAX's collectives and lax.ppermute only.
A program may use at most 64 MiB of HBM per device.

```python
import math
import jax
import jax.numpy as jnp
from jax import lax

D = 12288
HID = 24576
TOKENS = 512


def shard_levels(rng, shape, cuts, smallest, high):
    def one(dim, blocks):
        draws = jax.random.uniform(jax.random.fold_in(jax.random.fold_in(rng, 6), dim), (blocks,), jnp.float32, smallest / len(cuts), high / len(cuts))
        return jnp.repeat(jnp.exp(draws), shape[dim] // blocks).reshape((-1,) + (1,) * (len(shape) - dim - 1))

    factor_of = one(*cuts[0])
    for cut in cuts[1:]:
        factor_of = factor_of * one(*cut)
    return factor_of


def normal_values(own_key, extent, width, most, split=(), dtype=jnp.bfloat16):
    values = width * jax.random.normal(own_key, extent, jnp.float32)
    if split:
        values = values * shard_levels(own_key, extent, split, -0.22, 0.18)
    return jnp.clip(values, -most, most).astype(dtype)


def setup_inputs(seed: int = 0) -> dict:
    splits = jax.random.split(jax.random.key(seed), 5)
    tokens = normal_values(splits[0], (TOKENS, D), 1.0, 6.0, ((0, 64), (1, 4)))
    weight_in = normal_values(splits[1], (D, HID), D ** -0.5, 0.0546875, ((0, 4), (1, 64)))
    weight_out = normal_values(splits[2], (HID, D), HID ** -0.5, 0.0390625, ((0, 64), (1, 4)))
    cotangent = normal_values(splits[3], (TOKENS, D), 1.0, 6.0, ((0, 64), (1, 4)))
    return {"tokens": tokens, "weight_in": weight_in, "weight_out": weight_out, "cotangent": cotangent}


gelu_scale = math.sqrt(2.0 / math.pi)

def gelu_parts(pre):
    cubic = 0.044715 * pre * pre * pre
    tangent = jnp.tanh(gelu_scale * (pre + cubic))
    gelu_value = 0.5 * pre * (1.0 + tangent)
    gelu_slope = 0.5 * (1.0 + tangent) + 0.5 * pre * (1.0 - tangent * tangent) * gelu_scale * (1.0 + 3.0 * 0.044715 * pre * pre)
    return (gelu_value, gelu_slope)

def contract(left, right, left_dim, right_dim):
    return lax.dot_general(left, right, (((left_dim,), (right_dim,)), ((), ())), preferred_element_type=jnp.float32)

def reference(tokens, weight_in, weight_out, cotangent):
    pre = jnp.dot(tokens, weight_in, preferred_element_type=jnp.float32)
    gelu_value, gelu_slope = gelu_parts(pre)
    act = gelu_value.astype(jnp.bfloat16)
    grad_act = contract(cotangent, weight_out, 1, 1)
    grad_pre = (grad_act * gelu_slope).astype(jnp.bfloat16)
    grad_weight_out = contract(act, cotangent, 0, 0).astype(jnp.bfloat16)
    grad_weight_in = contract(tokens, grad_pre, 0, 0).astype(jnp.bfloat16)
    grad_tokens = contract(grad_pre, weight_in, 1, 1).astype(jnp.bfloat16)
    return (grad_tokens, grad_weight_in, grad_weight_out)
```

```python
import math

import jax
import jax.numpy as jnp
from jax import lax
from jax.sharding import PartitionSpec as P

gelu_scale = math.sqrt(2.0 / math.pi)
bf16, f32 = jnp.bfloat16, jnp.float32


def gelu_parts(pre):
    cubic = 0.044715 * pre * pre * pre
    tangent = jnp.tanh(gelu_scale * (pre + cubic))
    gelu_value = 0.5 * pre * (1.0 + tangent)
    gelu_slope = 0.5 * (1.0 + tangent) + 0.5 * pre * (1.0 - tangent * tangent) * gelu_scale * (
        1.0 + 3.0 * 0.044715 * pre * pre
    )
    return (gelu_value, gelu_slope)


def contract(left, right, left_dim, right_dim):
    return lax.dot_general(
        left, right, (((left_dim,), (right_dim,)), ((), ())), preferred_element_type=f32
    )


def move_y(value, step):
    return lax.ppermute(value, "wt", [(z * 4 + y, z * 4 + (y + step) % 4) for z in range(2) for y in range(4)])


def move_x(value, step):
    return lax.ppermute(value, "out", [(x * 2 + c, (x + step) % 4 * 2 + c) for x in range(4) for c in range(2)])


def move_z(value):
    return lax.ppermute(value, "wt", [(z * 4 + y, (1 - z) * 4 + y) for z in range(2) for y in range(4)])


def move_core(value):
    return lax.ppermute(value, "out", [(x * 2 + c, x * 2 + 1 - c) for x in range(4) for c in range(2)])


def move_inp(value, step):
    return lax.ppermute(value, "inp", [(i, (i + step) % 4) for i in range(4)])


def gather4(move, value):
    return [value] + [move(value, -step) for step in (1, 2, 3)]


def scatter4(move, blocks):
    total = blocks[0].astype(f32)
    for step in (1, 2, 3):
        total = total + move(blocks[step].astype(bf16), step).astype(f32)
    return total


def gather(value, first, second):
    value = jnp.concatenate([value, move_z(value)], 0)
    value = jnp.concatenate(gather4(first, value), 0)
    value = jnp.concatenate(gather4(second, value), 0)
    return jnp.concatenate([value, move_core(value)], 0)


def sum_inp(partial):
    me = lax.axis_index("inp")
    partial = partial.astype(bf16)
    block = lambda step: lax.dynamic_slice_in_dim(partial, (me + step) % 4 * 128, 128, 0)
    return scatter4(move_inp, [block(step) for step in range(4)])


def gather_inp(value):
    me = lax.axis_index("inp")
    full = jnp.zeros((512, value.shape[1]), value.dtype)
    for step, block in enumerate(gather4(move_inp, value)):
        full = lax.dynamic_update_slice_in_dim(full, block, (me + step) % 4 * 128, 0)
    return full


def shards(tokens, weight_in, weight_out, cotangent):
    token_full = gather(tokens, move_y, move_x)
    cotangent_full = gather(cotangent, move_x, move_y)
    cotangent_full = cotangent_full.reshape(2, 4, 4, 16, 3072).transpose(0, 2, 1, 3, 4).reshape(512, 3072)
    pre_rows = sum_inp(jnp.dot(token_full, weight_in, preferred_element_type=f32))
    grad_act_rows = sum_inp(contract(cotangent_full, weight_out, 1, 1))
    gelu_value, gelu_slope = gelu_parts(pre_rows)
    grad_pre = gather_inp((grad_act_rows * gelu_slope).astype(bf16))
    act = gather_inp(gelu_value.astype(bf16))
    grad_sum = contract(grad_pre, weight_in, 1, 1).astype(bf16)
    grad_weight_in = contract(token_full, grad_pre, 0, 0).astype(bf16)
    grad_weight_out = contract(act, cotangent_full, 0, 0).astype(bf16)
    half = grad_sum[:256].astype(f32) + move_core(grad_sum[256:]).astype(f32)
    half = half.reshape(4, 4, 16, 3072)
    left = half[..., :1536]
    left = scatter4(move_x, [left[d].reshape(64, 1536) for d in range(4)]).reshape(4, 16, 1536)
    left = scatter4(move_y, [left[d] for d in range(4)])
    right = half[..., 1536:]
    right = scatter4(move_y, [right[:, d].reshape(64, 1536) for d in range(4)]).reshape(4, 16, 1536)
    right = scatter4(move_x, [right[d] for d in range(4)])
    rows = jnp.concatenate([left, right], 1)
    rows = rows[:8] + move_z(rows[8:].astype(bf16)).astype(f32)
    return (rows.astype(bf16), grad_weight_in, grad_weight_out)


def solution(mesh):
    in_specs = (
        P(("wt", "out"), "inp"),
        P("inp", ("wt", "out")),
        P(("wt", "out"), "inp"),
        P(("wt", "out"), "inp"),
    )
    out_specs = (P(("wt", "out"), "inp"), P("inp", ("wt", "out")), P(("wt", "out"), "inp"))
    return jax.shard_map(shards, mesh=mesh, in_specs=in_specs, out_specs=out_specs, check_vma=False)
```

```python
import math

import jax
import jax.numpy as jnp
from jax import lax
from jax.sharding import PartitionSpec as P

gelu_scale = math.sqrt(2.0 / math.pi)
bf16, f32 = jnp.bfloat16, jnp.float32


def gelu_parts(pre):
    cubic = 0.044715 * pre * pre * pre
    tangent = jnp.tanh(gelu_scale * (pre + cubic))
    gelu_value = 0.5 * pre * (1.0 + tangent)
    gelu_slope = 0.5 * (1.0 + tangent) + 0.5 * pre * (1.0 - tangent * tangent) * gelu_scale * (
        1.0 + 3.0 * 0.044715 * pre * pre
    )
    return (gelu_value, gelu_slope)


def contract(left, right, left_dim, right_dim):
    return lax.dot_general(
        left, right, (((left_dim,), (right_dim,)), ((), ())), preferred_element_type=f32
    )


def even_pair(place):
    return place ^ 1


def odd_pair(place):
    return (place + 1) % 4 if place % 2 else (place - 1) % 4


def swap(value, partner):
    pairs = []
    for z in range(2):
        for y in range(4):
            for x in range(4):
                for core in range(2):
                    pz, py, px, pc = partner(z, y, x, core)
                    pairs.append(((z * 4 + y) * 8 + x * 2 + core, (pz * 4 + py) * 8 + px * 2 + pc))
    return lax.ppermute(value, ("wt", "out"), pairs)


def swap_z(value):
    return swap(value, lambda z, y, x, core: (1 - z, y, x, core))


def swap_core(value):
    return swap(value, lambda z, y, x, core: (z, y, x, 1 - core))


ORDERS = (
    (("x", even_pair), ("x", odd_pair), ("y", even_pair), ("y", odd_pair)),
    (("x", odd_pair), ("x", even_pair), ("y", odd_pair), ("y", even_pair)),
)


def swap_chip(value, chunk, step):
    orders = (ORDERS[chunk], ORDERS[chunk][2:] + ORDERS[chunk][:2])

    def partner(z, y, x, core):
        axis, pair = orders[core][step]
        return (z, pair(y), x, core) if axis == "y" else (z, y, pair(x), core)

    return swap(value, partner)


def move_inp(value, step):
    return lax.ppermute(value, "inp", [(i, (i + step) % 4) for i in range(4)])


def gather_chips(value, chunk):
    for step in range(4):
        value = jnp.concatenate([value, swap_chip(value, chunk, step)], 0)
    return value


def sum_chips(total, chunk):
    for step in (3, 2, 1, 0):
        rows = total.shape[0] // 2
        total = total[:rows] + swap_chip(total[rows:].astype(bf16), chunk, step).astype(f32)
    return total


def sum_inp(partial):
    me = lax.axis_index("inp")
    rows = partial.shape[0] // 4
    block = lambda step: lax.dynamic_slice_in_dim(partial, (me + step) % 4 * rows, rows, 0)
    total = block(0).astype(f32)
    for step in (1, 2, 3):
        total = total + move_inp(block(step), step).astype(f32)
    return total


def gather_inp(value):
    me = lax.axis_index("inp")
    rows = value.shape[0]
    full = jnp.zeros((4 * rows, value.shape[1]), value.dtype)
    full = lax.dynamic_update_slice_in_dim(full, value, me * rows, 0)
    for step in (1, 2, 3):
        full = lax.dynamic_update_slice_in_dim(full, move_inp(value, -step), (me + step) % 4 * rows, 0)
    return full


def shards(tokens, weight_in, weight_out, cotangent):
    own = jnp.concatenate([tokens, cotangent], 1)
    chunks = (own, swap_z(own))
    token_rows, cotangent_rows, act, grad_pre, sums = [], [], [], [], []
    partials = []
    for chunk in range(2):
        own = gather_chips(chunks[chunk], chunk)
        pieces = (own, swap_core(own))
        token_rows += [piece[:, :3072] for piece in pieces]
        cotangent_rows += [piece[:, 3072:] for piece in pieces]
        partials.append(
            jnp.concatenate(
                [
                    jnp.concatenate(
                        [
                            jnp.dot(piece[:, :3072], weight_in, preferred_element_type=f32).astype(bf16),
                            contract(piece[:, 3072:], weight_out, 1, 1).astype(bf16),
                        ],
                        1,
                    )
                    for piece in pieces
                ],
                0,
            )
        )
    for chunk in range(2):
        rows = sum_inp(partials[chunk])
        gelu_value, gelu_slope = gelu_parts(rows[:, :384])
        rows = jnp.concatenate([gelu_value, rows[:, 384:] * gelu_slope], 1).astype(bf16)
        rows = gather_inp(rows)
        act.append(rows[:, :384])
        grad_pre.append(rows[:, 384:])
        sums.append(contract(rows[:, 384:], weight_in, 1, 1))
    totals = []
    for chunk in range(2):
        total = sums[chunk][:128] + swap_core(sums[chunk][128:].astype(bf16)).astype(f32)
        totals.append(sum_chips(total, chunk))
    grad_tokens = totals[0] + swap_z(totals[1].astype(bf16)).astype(f32)
    grad_weight_in = contract(jnp.concatenate(token_rows, 0), jnp.concatenate(grad_pre, 0), 0, 0)
    grad_weight_out = contract(jnp.concatenate(act, 0), jnp.concatenate(cotangent_rows, 0), 0, 0)
    return (grad_tokens.astype(bf16), grad_weight_in.astype(bf16), grad_weight_out.astype(bf16))


def solution(mesh):
    in_specs = (
        P(("wt", "out"), "inp"),
        P("inp", ("wt", "out")),
        P(("wt", "out"), "inp"),
        P(("wt", "out"), "inp"),
    )
    out_specs = (P(("wt", "out"), "inp"), P("inp", ("wt", "out")), P(("wt", "out"), "inp"))
    return jax.shard_map(shards, mesh=mesh, in_specs=in_specs, out_specs=out_specs, check_vma=False)
```

```python
import math

import jax
import jax.numpy as jnp
from jax import lax
from jax.experimental import pallas as pl
from jax.experimental.pallas import tpu as pltpu
from jax.sharding import PartitionSpec as P

gelu_scale = math.sqrt(2.0 / math.pi)
bf16, f32 = jnp.bfloat16, jnp.float32


def gelu_parts(pre):
    cubic = 0.044715 * pre * pre * pre
    tangent = jnp.tanh(gelu_scale * (pre + cubic))
    gelu_value = 0.5 * pre * (1.0 + tangent)
    gelu_slope = 0.5 * (1.0 + tangent) + 0.5 * pre * (1.0 - tangent * tangent) * gelu_scale * (
        1.0 + 3.0 * 0.044715 * pre * pre
    )
    return (gelu_value, gelu_slope)


def contract(left, right, left_dim, right_dim):
    return lax.dot_general(
        left, right, (((left_dim,), (right_dim,)), ((), ())), preferred_element_type=f32
    )


def move(value, target):
    pairs = []
    for z in range(2):
        for y in range(4):
            for x in range(4):
                for core in range(2):
                    tz, ty, tx, tc = target(z, y, x, core)
                    pairs.append(((z * 4 + y) * 8 + x * 2 + core, (tz * 4 + ty) * 8 + tx * 2 + tc))
    return lax.ppermute(value, ("wt", "out"), pairs)


def swap_z(value):
    return move(value, lambda z, y, x, core: (1 - z, y, x, core))


def swap_core(value):
    return move(value, lambda z, y, x, core: (z, y, x, 1 - core))


def move_chip(value, stage, step):
    def target(z, y, x, core):
        along_x = stage != core
        return (z, y, (x + step) % 4, core) if along_x else (z, (y + step) % 4, x, core)

    return move(value, target)


def gather4(value, stage):
    return [value] + [move_chip(value, stage, -step) for step in (2, 1, 3)]


def sum4(total, stage):
    rows = total.shape[0] // 4
    out = total[:rows].astype(f32)
    for place, step in enumerate((2, 1, 3)):
        block = total[(place + 1) * rows : (place + 2) * rows]
        out = out + move_chip(block.astype(bf16), stage, step).astype(f32)
    return out


def move_inp(value, step):
    return lax.ppermute(value, "inp", [(i, (i + step) % 4) for i in range(4)])


def gather_inp(value):
    return [value] + [move_inp(value, -step) for step in (2, 1, 3)]


def call(kernel, out_shapes, operands, later=(), scratch=()):
    whole = pl.BlockSpec(memory_space=pltpu.VMEM)

    def body(*refs):
        kernel(*refs[: len(operands)], *refs[len(operands) + len(later) :])

    return pl.pallas_call(
        body,
        out_shape=[jax.ShapeDtypeStruct(shape, bf16) for shape in out_shapes],
        in_specs=[whole] * len(operands) + [pl.BlockSpec(memory_space=pl.ANY)] * len(later),
        out_specs=[whole] * len(out_shapes),
        scratch_shapes=list(scratch),
        cost_estimate=pl.CostEstimate(flops=0, bytes_accessed=0, transcendentals=0),
        compiler_params=pltpu.CompilerParams(vmem_limit_bytes=16 * 2**20),
    )(*operands, *later)


def pair_kernel(token, cotangent, out):
    out[:, :3072] = token[...]
    out[:, 3072:] = cotangent[...]


def rows16_kernel(own, other, out):
    out[...] = jnp.concatenate([own[...].astype(f32), other[...].astype(f32)], 0).astype(bf16)


def stack_kernel(*refs):
    rows = refs[0].shape[0]
    for place, piece in enumerate(refs[:-1]):
        refs[-1][pl.ds(place * rows, rows), :] = piece[...]


def stack(pieces, later=()):
    rows, columns = pieces[0].shape
    return call(stack_kernel, [(4 * rows, columns)], pieces, later)[0]


def partials(rows, weight_in, weight_out):
    pre = jnp.dot(rows[:, :3072], weight_in[...], preferred_element_type=f32).astype(bf16)
    return pre, contract(rows[:, 3072:], weight_out[...], 1, 1).astype(bf16)


def own_kernel(rows, weight_in, weight_out, out):
    out[:, :384], out[:, 384:] = partials(rows, weight_in, weight_out)


def other_kernel(rows, weight_in, weight_out, own, *outs):
    outs, full = outs[:4], outs[4]
    full[:256, :] = own[...]
    full[256:, :384], full[256:, 384:] = partials(rows, weight_in, weight_out)
    me = lax.axis_index("inp")
    for step, out in zip((0, 2, 1, 3), outs):
        out[...] = full[pl.ds(pl.multiple_of(lax.rem(me + step, 4) * 128, 128), 128), :]


def gelu_kernel(own, first, second, third, act, grad_pre):
    total = own[...].astype(f32) + first[...].astype(f32) + second[...].astype(f32) + third[...].astype(f32)
    gelu_value, gelu_slope = gelu_parts(total[:, :384])
    act[...] = gelu_value.astype(bf16)
    grad_pre[...] = (total[:, 384:] * gelu_slope).astype(bf16)


def place_kernel(*refs):
    me = lax.axis_index("inp")
    for step, block in zip((0, 2, 1, 3), refs[:4]):
        refs[4][pl.ds(pl.multiple_of(lax.rem(me + step, 4) * 128, 128), 128), :] = block[...]


def place(blocks, later=()):
    return call(place_kernel, [(512, 384)], blocks, later)[0]


def copy_kernel(value, out):
    out[...] = value[...]


def after(value, *later):
    return call(copy_kernel, [value.shape], (value,), later)[0]


def shards(tokens, weight_in, weight_out, cotangent):
    rows = call(pair_kernel, [(8, 6144)], (tokens, cotangent))[0]
    rows = call(rows16_kernel, [(16, 6144)], (rows, swap_z(rows)))[0]
    rows = stack(gather4(rows, 0))
    own = stack(gather4(rows, 1))
    other = swap_core(own)
    weights = (weight_in, weight_out)
    partial = call(own_kernel, [(256, 768)], (own, *weights))[0]
    blocks = call(other_kernel, [(128, 768)] * 4, (other, *weights, partial), scratch=[pltpu.VMEM((512, 768), bf16)])
    moved = [move_inp(block, step) for step, block in zip((2, 1, 3), blocks[1:])]
    act, grad_pre = call(gelu_kernel, [(128, 384)] * 2, (blocks[0], *moved))
    grad_pre = place(gather_inp(grad_pre))
    sent = contract(grad_pre[256:], weight_in, 1, 1).astype(bf16)
    act = gather_inp(after(act, sent))
    total = contract(grad_pre[:256], weight_in, 1, 1) + swap_core(sent).astype(f32)
    grad_weight_in = contract(own[:, :3072], grad_pre[:256], 0, 0) + contract(other[:, :3072], grad_pre[256:], 0, 0)
    total = sum4(total, 1)
    total = sum4(total, 0)
    last = total[8:].astype(bf16)
    grad_tokens = total[:8] + swap_z(last).astype(f32)
    act = place(act)
    grad_weight_out = contract(act[:256], own[:, 3072:], 0, 0) + contract(act[256:], other[:, 3072:], 0, 0)
    return (grad_tokens.astype(bf16), grad_weight_in.astype(bf16), grad_weight_out.astype(bf16))


def solution(mesh):
    in_specs = (
        P(("wt", "out"), "inp"),
        P("inp", ("wt", "out")),
        P(("wt", "out"), "inp"),
        P(("wt", "out"), "inp"),
    )
    out_specs = (P(("wt", "out"), "inp"), P("inp", ("wt", "out")), P(("wt", "out"), "inp"))
    return jax.shard_map(shards, mesh=mesh, in_specs=in_specs, out_specs=out_specs, check_vma=False)
```

```python
import math

import jax
import jax.numpy as jnp
from jax import lax
from jax.experimental import pallas as pl
from jax.experimental.pallas import tpu as pltpu
from jax.sharding import PartitionSpec as P

gelu_scale = math.sqrt(2.0 / math.pi)
bf16, f32 = jnp.bfloat16, jnp.float32


def gelu_parts(pre):
    cubic = 0.044715 * pre * pre * pre
    tangent = jnp.tanh(gelu_scale * (pre + cubic))
    gelu_value = 0.5 * pre * (1.0 + tangent)
    gelu_slope = 0.5 * (1.0 + tangent) + 0.5 * pre * (1.0 - tangent * tangent) * gelu_scale * (
        1.0 + 3.0 * 0.044715 * pre * pre
    )
    return (gelu_value, gelu_slope)


def contract(left, right, left_dim, right_dim):
    return lax.dot_general(
        left, right, (((left_dim,), (right_dim,)), ((), ())), preferred_element_type=f32
    )


def move(value, target):
    pairs = []
    for z in range(2):
        for y in range(4):
            for x in range(4):
                for core in range(2):
                    tz, ty, tx, tc = target(z, y, x, core)
                    pairs.append(((z * 4 + y) * 8 + x * 2 + core, (tz * 4 + ty) * 8 + tx * 2 + tc))
    return lax.ppermute(value, ("wt", "out"), pairs)


def swap_z(value):
    return move(value, lambda z, y, x, core: (1 - z, y, x, core))


def swap_core(value):
    return move(value, lambda z, y, x, core: (z, y, x, 1 - core))


def move_chip(value, stage, step):
    def target(z, y, x, core):
        along_x = stage != core
        return (z, y, (x + step) % 4, core) if along_x else (z, (y + step) % 4, x, core)

    return move(value, target)


def gather4(value, stage):
    return [value] + [move_chip(value, stage, -step) for step in (2, 1, 3)]


def scatter(blocks, stage, steps):
    return [move_chip(block, stage, step) for block, step in zip(blocks, steps)]


def move_inp(value, step):
    return lax.ppermute(value, "inp", [(i, (i + step) % 4) for i in range(4)])


def gather_inp(value):
    return [value] + [move_inp(value, -step) for step in (2, 1, 3)]


WHOLE = pl.BlockSpec(memory_space=pltpu.VMEM)


def call(kernel, outs, operands, later=(), scratch=(), in_specs=None, **kwargs):
    def body(*refs):
        kernel(*refs[: len(operands)], *refs[len(operands) + len(later) :])

    in_specs = in_specs or [WHOLE] * len(operands)
    return pl.pallas_call(
        body,
        out_shape=[out if isinstance(out, jax.ShapeDtypeStruct) else jax.ShapeDtypeStruct(out, bf16) for out in outs],
        in_specs=in_specs + [pl.BlockSpec(memory_space=pl.ANY)] * len(later),
        out_specs=[WHOLE] * len(outs),
        scratch_shapes=list(scratch),
        cost_estimate=pl.CostEstimate(flops=0, bytes_accessed=0, transcendentals=0),
        compiler_params=pltpu.CompilerParams(vmem_limit_bytes=16 * 2**20),
        **kwargs,
    )(*operands, *later)


ANYWHERE = pl.BlockSpec(memory_space=pl.ANY)


def pair_kernel(token, cotangent, out, sems):
    copies = [
        pltpu.make_async_copy(value, out.at[:, pl.ds(place * 3072, 3072)], sems.at[place])
        for place, value in enumerate((token, cotangent))
    ]
    for copy in copies:
        copy.start()
    for copy in copies:
        copy.wait()


def weight_in_kernel(own, other, out, sem):
    copy = pltpu.make_async_copy(own, out.at[:, pl.ds(0, 384)], sem)
    copy.start()
    out[:, 384:] = other[...]
    copy.wait()


def weight_out_kernel(own, other, out, sem):
    copy = pltpu.make_async_copy(own, out.at[pl.ds(0, 384), :], sem)
    copy.start()
    out[384:, :] = other[...]
    copy.wait()


def rows16_kernel(own, other, out):
    out[...] = jnp.concatenate([own[...].astype(f32), other[...].astype(f32)], 0).astype(bf16)


def stack_kernel(*refs):
    start = 0
    for piece in refs[:-1]:
        refs[-1][pl.ds(start, piece.shape[0]), :] = piece[...]
        start += piece.shape[0]


def stack(pieces, later=()):
    rows = sum(piece.shape[0] for piece in pieces)
    return call(stack_kernel, [(rows, pieces[0].shape[1])], pieces, later)[0]


def halves_kernel(*refs):
    whole, top, bottom = refs[4:]
    stack_kernel(*refs[:4], whole)
    stack_kernel(*refs[:2], top)
    stack_kernel(*refs[2:4], bottom)


def partial_kernel(rows, weight_in, weight_out, *outs):
    outs, full = outs[:4], outs[4]
    quarter = rows.shape[0] // 4
    full[:, :768] = jnp.dot(rows[:, :3072], weight_in[...], preferred_element_type=f32).astype(bf16)
    full[:, 768:] = contract(rows[:, 3072:], weight_out[...], 1, 1).astype(bf16)
    me = lax.axis_index("inp")
    for step, out in zip((0, 2, 1, 3), outs):
        out[...] = full[pl.ds(pl.multiple_of(lax.rem(me + step, 4) * quarter, quarter), quarter), :]


def sum_inp(rows, weights, later=()):
    blocks = call(
        partial_kernel,
        [(rows.shape[0] // 4, 1536)] * 4,
        (rows, *weights),
        later,
        scratch=[pltpu.VMEM((rows.shape[0], 1536), bf16)],
    )
    return [blocks[0]] + [move_inp(block, step) for step, block in zip((2, 1, 3), blocks[1:])]


def gelu_kernel(*refs):
    own_act, other_act, grad_pre = refs[8:]
    start = 0
    for blocks in (refs[:4], refs[4:8]):
        total = sum(block[...].astype(f32) for block in blocks[1:]) + blocks[0][...].astype(f32)
        rows = pl.ds(start, total.shape[0])
        gelu_value, gelu_slope = gelu_parts(total[:, :768])
        own_act[rows, :] = gelu_value[:, :384].astype(bf16)
        other_act[rows, :] = gelu_value[:, 384:].astype(bf16)
        grad_pre[rows, :] = (total[:, 768:] * gelu_slope).astype(bf16)
        start += total.shape[0]


CHUNKS = ((0, 48), (48, 16))


def place_grad_kernel(*refs):
    out, sent = refs[4:]
    me = lax.axis_index("inp")
    for step, block in zip((0, 2, 1, 3), refs[:4]):
        place = lax.rem(me + step, 4)
        for start, rows in CHUNKS:
            to = pl.ds(pl.multiple_of(4 * start + place * rows, 16), rows)
            out[to, :] = block[start : start + rows, :]
            sent[to, :] = block[start : start + rows, 384:]


def place_act_kernel(*refs):
    me = lax.axis_index("inp")
    for step, block in zip((0, 2, 1, 3), refs[:4]):
        place = lax.rem(me + step, 4)
        for core in range(2):
            for start, rows in CHUNKS:
                to = pl.ds(pl.multiple_of(256 * core + 4 * start + place * rows, 16), rows)
                refs[4][to, :] = block[64 * core + start : 64 * core + start + rows, :]


def split_kernel(value, total, *blocks):
    total[...] = value[:64, :]
    for place, block in enumerate(blocks):
        block[...] = value[pl.ds(64 * place + 64, 64), :].astype(bf16)


def sum_kernel(own, first, second, third, total, *blocks):
    rows = total.shape[0]
    for place, out in enumerate((total, *blocks)):
        part = pl.ds(place * rows, rows)
        value = own[part, :] + first[part, :].astype(f32) + second[part, :].astype(f32) + third[part, :].astype(f32)
        out[...] = value.astype(out.dtype)


def last_kernel(own, first, second, third, total, sent):
    value = own[...] + first[...].astype(f32) + second[...].astype(f32) + third[...].astype(f32)
    total[...] = value[:8, :]
    sent[...] = value[8:, :].astype(bf16)


def copy_kernel(value, out):
    out[...] = value[...]


def after(value, *later):
    return call(copy_kernel, [value.shape], (value,), later)[0]


def shards(tokens, weight_in, weight_out, cotangent):
    dma = pltpu.SemaphoreType.DMA
    rows = call(
        pair_kernel, [(8, 6144)], (tokens, cotangent), in_specs=[ANYWHERE] * 2, scratch=[dma((2,))]
    )[0]
    rows_z = swap_z(rows)
    both = [ANYWHERE, WHOLE]
    weights = (
        call(weight_in_kernel, [(3072, 768)], (weight_in, swap_core(weight_in)), in_specs=both, scratch=[dma(())])[0],
        call(weight_out_kernel, [(768, 3072)], (weight_out, swap_core(weight_out)), in_specs=both, scratch=[dma(())])[0],
    )
    rows = call(rows16_kernel, [(16, 6144)], (rows, rows_z), weights)[0]
    rows, top, bottom = call(halves_kernel, [(64, 6144), (32, 6144), (32, 6144)], gather4(rows, 0))
    up = [move_chip(half, 1, -1) for half in (top, bottom)]
    down = [move_chip(half, 1, 1) for half in (top, bottom)]
    near_rows = stack((rows, *up, *down))
    far = [move_chip(up[0], 1, -1), move_chip(down[1], 1, 1)]
    near = sum_inp(near_rows, weights)
    far_rows = stack(far, near[:1])
    far = sum_inp(far_rows, weights)
    own_act, other_act, grad_pre = call(gelu_kernel, [(64, 384), (64, 384), (64, 768)], (*near, *far))
    act = stack((own_act, swap_core(other_act)))
    grad_pre, sent = call(
        place_grad_kernel, [(256, 768), (256, 384)], gather_inp(grad_pre), (act,)
    )
    total, *blocks = call(
        split_kernel,
        [jax.ShapeDtypeStruct((64, 3072), f32)] + [(64, 3072)] * 3,
        (contract(grad_pre, weights[0], 1, 1),),
    )
    own = stack((near_rows, far_rows), blocks[:1])
    other = swap_core(own)
    act = gather_inp(after(act, blocks[0]))
    grad_pre = (after(grad_pre, blocks[0])[:, :384], swap_core(after(sent, blocks[0])))
    total, *blocks = call(
        sum_kernel,
        [jax.ShapeDtypeStruct((16, 3072), f32)] + [(16, 3072)] * 3,
        (total, *scatter(blocks, 1, (1, 3, 2))),
        (grad_pre[1], act[1], act[2], other),
    )
    grad_weight_in = contract(own[:, :3072], grad_pre[0], 0, 0) + contract(other[:, :3072], grad_pre[1], 0, 0)
    grad_weight_in = grad_weight_in.astype(bf16)
    total, last = call(
        last_kernel,
        [jax.ShapeDtypeStruct((8, 3072), f32), (8, 3072)],
        (total, *scatter(blocks, 0, (2, 1, 3))),
        (grad_weight_in,),
    )
    grad_tokens = total + swap_z(last).astype(f32)
    act = call(place_act_kernel, [(512, 384)], act, (last,))[0]
    grad_weight_out = contract(act[:256], own[:, 3072:], 0, 0) + contract(act[256:], other[:, 3072:], 0, 0)
    return (grad_tokens.astype(bf16), grad_weight_in, grad_weight_out.astype(bf16))


def solution(mesh):
    in_specs = (
        P(("wt", "out"), "inp"),
        P("inp", ("wt", "out")),
        P(("wt", "out"), "inp"),
        P(("wt", "out"), "inp"),
    )
    out_specs = (P(("wt", "out"), "inp"), P("inp", ("wt", "out")), P(("wt", "out"), "inp"))
    return jax.shard_map(shards, mesh=mesh, in_specs=in_specs, out_specs=out_specs, check_vma=False)
```

```python
import math

import jax
import jax.numpy as jnp
from jax import lax
from jax.experimental import pallas as pl
from jax.experimental.pallas import tpu as pltpu
from jax.sharding import PartitionSpec as P

gelu_scale = math.sqrt(2.0 / math.pi)
bf16, f32 = jnp.bfloat16, jnp.float32


def gelu_parts(pre):
    cubic = 0.044715 * pre * pre * pre
    tangent = jnp.tanh(gelu_scale * (pre + cubic))
    gelu_value = 0.5 * pre * (1.0 + tangent)
    gelu_slope = 0.5 * (1.0 + tangent) + 0.5 * pre * (1.0 - tangent * tangent) * gelu_scale * (
        1.0 + 3.0 * 0.044715 * pre * pre
    )
    return (gelu_value, gelu_slope)


def contract(left, right, left_dim, right_dim):
    return lax.dot_general(
        left, right, (((left_dim,), (right_dim,)), ((), ())), preferred_element_type=f32
    )


def move(value, target):
    pairs = []
    for z in range(2):
        for y in range(4):
            for x in range(4):
                for core in range(2):
                    tz, ty, tx, tc = target(z, y, x, core)
                    pairs.append(((z * 4 + y) * 8 + x * 2 + core, (tz * 4 + ty) * 8 + tx * 2 + tc))
    return lax.ppermute(value, ("wt", "out"), pairs)


def swap_z(value):
    return move(value, lambda z, y, x, core: (1 - z, y, x, core))


def swap_core(value):
    return move(value, lambda z, y, x, core: (z, y, x, 1 - core))


def move_chip(value, stage, step):
    def target(z, y, x, core):
        along_x = stage != core
        return (z, y, (x + step) % 4, core) if along_x else (z, (y + step) % 4, x, core)

    return move(value, target)


def gather4(value, stage):
    return [value] + [move_chip(value, stage, -step) for step in (2, 1, 3)]


def scatter(blocks, stage, steps):
    return [move_chip(block, stage, step) for block, step in zip(blocks, steps)]


def move_inp(value, step):
    return lax.ppermute(value, "inp", [(i, (i + step) % 4) for i in range(4)])


def gather_inp(value):
    return [value] + [move_inp(value, -step) for step in (2, 1, 3)]


WHOLE = pl.BlockSpec(memory_space=pltpu.VMEM)


def call(kernel, outs, operands, later=(), scratch=(), in_specs=None, **kwargs):
    def body(*refs):
        kernel(*refs[: len(operands)], *refs[len(operands) + len(later) :])

    in_specs = in_specs or [WHOLE] * len(operands)
    return pl.pallas_call(
        body,
        out_shape=[out if isinstance(out, jax.ShapeDtypeStruct) else jax.ShapeDtypeStruct(out, bf16) for out in outs],
        in_specs=in_specs + [pl.BlockSpec(memory_space=pl.ANY)] * len(later),
        out_specs=[WHOLE] * len(outs),
        scratch_shapes=list(scratch),
        cost_estimate=pl.CostEstimate(flops=0, bytes_accessed=0, transcendentals=0),
        compiler_params=pltpu.CompilerParams(vmem_limit_bytes=16 * 2**20),
        **kwargs,
    )(*operands, *later)


ANYWHERE = pl.BlockSpec(memory_space=pl.ANY)


def pair_kernel(token, cotangent, out, sems):
    copies = [
        pltpu.make_async_copy(value, out.at[:, pl.ds(place * 3072, 3072)], sems.at[place])
        for place, value in enumerate((token, cotangent))
    ]
    for copy in copies:
        copy.start()
    for copy in copies:
        copy.wait()


def weight_in_kernel(own, other, out, sem):
    copy = pltpu.make_async_copy(own, out.at[:, pl.ds(0, 384)], sem)
    copy.start()
    out[:, 384:] = other[...]
    copy.wait()


def weight_out_kernel(own, other, out, sem):
    copy = pltpu.make_async_copy(own, out.at[pl.ds(0, 384), :], sem)
    copy.start()
    out[384:, :] = other[...]
    copy.wait()


def rows16_kernel(own, other, out):
    out[...] = jnp.concatenate([own[...].astype(f32), other[...].astype(f32)], 0).astype(bf16)


def stack_kernel(*refs):
    start = 0
    for piece in refs[:-1]:
        refs[-1][pl.ds(start, piece.shape[0]), :] = piece[...]
        start += piece.shape[0]


def stack(pieces, later=()):
    rows = sum(piece.shape[0] for piece in pieces)
    return call(stack_kernel, [(rows, pieces[0].shape[1])], pieces, later)[0]


def halves_kernel(*refs):
    whole, top, bottom = refs[4:]
    stack_kernel(*refs[:4], whole)
    stack_kernel(*refs[:2], top)
    stack_kernel(*refs[2:4], bottom)


def partial_kernel(rows, weight_in, weight_out, *outs):
    outs, full = outs[:4], outs[4]
    quarter = rows.shape[0] // 4
    full[:, :768] = jnp.dot(rows[:, :3072], weight_in[...], preferred_element_type=f32).astype(bf16)
    full[:, 768:] = contract(rows[:, 3072:], weight_out[...], 1, 1).astype(bf16)
    me = lax.axis_index("inp")
    for step, out in zip((0, 2, 1, 3), outs):
        out[...] = full[pl.ds(pl.multiple_of(lax.rem(me + step, 4) * quarter, quarter), quarter), :]


def sum_inp(rows, weights, later=()):
    blocks = call(
        partial_kernel,
        [(rows.shape[0] // 4, 1536)] * 4,
        (rows, *weights),
        later,
        scratch=[pltpu.VMEM((rows.shape[0], 1536), bf16)],
    )
    return [blocks[0]] + [move_inp(block, step) for step, block in zip((2, 1, 3), blocks[1:])]


def gelu_kernel(*refs):
    own_act, other_act, grad_pre = refs[8:]
    start = 0
    for blocks in (refs[:4], refs[4:8]):
        total = sum(block[...].astype(f32) for block in blocks[1:]) + blocks[0][...].astype(f32)
        rows = pl.ds(start, total.shape[0])
        gelu_value, gelu_slope = gelu_parts(total[:, :768])
        own_act[rows, :] = gelu_value[:, :384].astype(bf16)
        other_act[rows, :] = gelu_value[:, 384:].astype(bf16)
        grad_pre[rows, :] = (total[:, 768:] * gelu_slope).astype(bf16)
        start += total.shape[0]


CHUNKS = ((0, 48), (48, 16))


def place_grad_kernel(*refs):
    out, sent = refs[4:]
    me = lax.axis_index("inp")
    for step, block in zip((0, 2, 1, 3), refs[:4]):
        place = lax.rem(me + step, 4)
        for start, rows in CHUNKS:
            to = pl.ds(pl.multiple_of(4 * start + place * rows, 16), rows)
            out[to, :] = block[start : start + rows, :]
            sent[to, :] = block[start : start + rows, 384:]


def place_act_kernel(*refs):
    me = lax.axis_index("inp")
    for step, block in zip((0, 2, 1, 3), refs[:4]):
        place = lax.rem(me + step, 4)
        for core in range(2):
            for start, rows in CHUNKS:
                to = pl.ds(pl.multiple_of(256 * core + 4 * start + place * rows, 16), rows)
                refs[4][to, :] = block[64 * core + start : 64 * core + start + rows, :]


def split_kernel(value, total, *blocks):
    total[...] = value[:64, :]
    for place, block in enumerate(blocks):
        block[...] = value[pl.ds(64 * place + 64, 64), :].astype(bf16)


def sum_kernel(own, first, second, third, total, *blocks):
    rows = total.shape[0]
    for place, out in enumerate((total, *blocks)):
        part = pl.ds(place * rows, rows)
        value = own[part, :] + first[part, :].astype(f32) + second[part, :].astype(f32) + third[part, :].astype(f32)
        out[...] = value.astype(out.dtype)


def last_kernel(own, first, second, third, total, sent):
    value = own[...] + first[...].astype(f32) + second[...].astype(f32) + third[...].astype(f32)
    total[...] = value[:8, :]
    sent[...] = value[8:, :].astype(bf16)


def copy_kernel(value, out):
    out[...] = value[...]


def after(value, *later):
    return call(copy_kernel, [value.shape], (value,), later)[0]


def shards(tokens, weight_in, weight_out, cotangent):
    dma = pltpu.SemaphoreType.DMA
    rows = call(
        pair_kernel, [(8, 6144)], (tokens, cotangent), in_specs=[ANYWHERE] * 2, scratch=[dma((2,))]
    )[0]
    rows_z = swap_z(rows)
    both = [ANYWHERE, WHOLE]
    weights = (
        call(weight_in_kernel, [(3072, 768)], (weight_in, swap_core(weight_in)), in_specs=both, scratch=[dma(())])[0],
        call(weight_out_kernel, [(768, 3072)], (weight_out, swap_core(weight_out)), in_specs=both, scratch=[dma(())])[0],
    )
    rows = call(rows16_kernel, [(16, 6144)], (rows, rows_z), weights)[0]
    rows, top, bottom = call(halves_kernel, [(64, 6144), (32, 6144), (32, 6144)], gather4(rows, 0))
    up = [move_chip(half, 1, -1) for half in (top, bottom)]
    down = [move_chip(half, 1, 1) for half in (top, bottom)]
    near_rows = stack((rows, *up, *down))
    far = [move_chip(up[0], 1, -1), move_chip(down[1], 1, 1)]
    near = sum_inp(near_rows, weights)
    far_rows = stack(far, near[:1])
    far = sum_inp(far_rows, weights)
    own_act, other_act, grad_pre = call(gelu_kernel, [(64, 384), (64, 384), (64, 768)], (*near, *far))
    act = stack((own_act, swap_core(other_act)))
    grad_pre, sent = call(
        place_grad_kernel, [(256, 768), (256, 384)], gather_inp(grad_pre), (act,)
    )
    total, *blocks = call(
        split_kernel,
        [jax.ShapeDtypeStruct((64, 3072), f32)] + [(64, 3072)] * 3,
        (contract(grad_pre, weights[0], 1, 1),),
    )
    own = stack((near_rows, far_rows), blocks[:1])
    other = swap_core(own)
    act = gather_inp(after(act, blocks[0]))
    grad_pre = (after(grad_pre, blocks[0])[:, :384], swap_core(after(sent, blocks[0])))
    total, *blocks = call(
        sum_kernel,
        [jax.ShapeDtypeStruct((16, 3072), f32)] + [(16, 3072)] * 3,
        (total, *scatter(blocks, 1, (1, 3, 2))),
        (grad_pre[1], other),
    )
    grad_weight_in = contract(own[:, :3072], grad_pre[0], 0, 0) + contract(other[:, :3072], grad_pre[1], 0, 0)
    grad_weight_in = grad_weight_in.astype(bf16)
    total, last = call(
        last_kernel,
        [jax.ShapeDtypeStruct((8, 3072), f32), (8, 3072)],
        (total, *scatter(blocks, 0, (2, 1, 3))),
        (grad_weight_in,),
    )
    grad_tokens = total + swap_z(last).astype(f32)
    act = call(place_act_kernel, [(512, 384)], act, (last,))[0]
    grad_weight_out = contract(act[:256], own[:, 3072:], 0, 0) + contract(act[256:], other[:, 3072:], 0, 0)
    return (grad_tokens.astype(bf16), grad_weight_in, grad_weight_out.astype(bf16))


def solution(mesh):
    in_specs = (
        P(("wt", "out"), "inp"),
        P("inp", ("wt", "out")),
        P(("wt", "out"), "inp"),
        P(("wt", "out"), "inp"),
    )
    out_specs = (P(("wt", "out"), "inp"), P("inp", ("wt", "out")), P(("wt", "out"), "inp"))
    return jax.shard_map(shards, mesh=mesh, in_specs=in_specs, out_specs=out_specs, check_vma=False)
```
